32 devices in a mesh: groups: 2 (over x), chan: 16 (over z, y, core).
Axes of the slice: x: 2, y: 2, z: 4, core: 2. Of those that a mesh axis runs over, the one named last changes fastest.
Arguments:
- strain: float32 [256, 72704], P(('groups', 'chan')), parts along dimension 0, may hold values from -32 to 32, as said below
- window: float32 [8, 1024], replicated, may hold values from -0.0625 to 0.0625
- row_channel: int32 [256], P('groups'), parts along dimension 0, may hold values from 0 to 127, as said below
- pair_ids: int32 [2, 2048], P(None, ('groups', 'chan')), parts along dimension 1, may hold values from 0 to 127, as said below
- pair_count: int32 [32], P(('groups', 'chan')), parts along dimension 0, may hold values from 1 to 64, as said below
- auto_prev: float32 [1024, 128], P(('groups', 'chan')), parts along dimension 0, may hold values from 0.5 to 4
- cross_prev: float32 [2, 1024, 64], P(None, ('groups', 'chan')), parts along dimension 1, may hold values from -4 to 4
Outputs:
- transfer: float32 [2, 1024, 64], P(None, ('groups', 'chan')), parts along dimension 1
- cross_new: float32 [2, 1024, 64], P(None, ('groups', 'chan')), parts along dimension 1
- auto_new: float32 [1024, 128], P(('groups', 'chan')), parts along dimension 0
The draws below stay inside these ranges and needn't reach their ends.
There are 2 independent parts, one for each index of `groups`. The reference program is written for one: setup_inputs(seed, part) draws one part's arguments, and reference() takes and returns one part's arrays. A program takes and returns all parts, laid end to end along the dimension named above; an argument that names none is the same for every part. Nothing has to cross between parts.
Inputs may be any that keep to these rules, and one draw needn't show every extreme that they name: `row_channel`: each channel appears in exactly one row. `pair_ids`: rows i and j of a slot name different channels. Over all 64 slots of one owner, the distinct channels named that lie in the rows of any one index of chan number at most 4, and exactly 4 for some index and owner. `pair_count`: some owner has all 64 slots live. `strain`: samples are a sum of a part common to all channels, a delayed part with a gain of each channel, and independent noise.
All inputs are finite; a program needn't handle non-finite values.
Results may differ from the reference program's by a relative error of at most 0.0003.
Values sent between devices are 32-bit elements; how exact they have to be, the bound alone decides.
A program may use at most 64 MiB of HBM per device.

```python
import math
import jax
import jax.numpy as jnp
from jax import lax

FFT_LEN = 1024
TAPS = 8
CH_DEV = 8
FRAMES = 64
PAIR_DEV = 64
CAP = 4
BINS = 512
BIN_DEV = 32
CHANNELS = 128
SAMPLES = 72704
N_CHAN = 16


def draw_strain(key, part):
    gains = jnp.exp(jax.random.uniform(jax.random.fold_in(key, 1), (CHANNELS, 1), jnp.float32, math.log(0.5), math.log(2.0)))
    wave_gain = jax.random.truncated_normal(jax.random.fold_in(key, 2), -3.0, 3.0, (CHANNELS, 1), jnp.float32)
    delays = jax.random.randint(jax.random.fold_in(key, 3), (CHANNELS,), 0, FFT_LEN // 4)
    extent = SAMPLES + FFT_LEN // 4
    shared_trace = jax.random.truncated_normal(jax.random.fold_in(key, 4), -4.0, 4.0, (SAMPLES,), jnp.float32)
    wave_trace = jax.random.truncated_normal(jax.random.fold_in(key, 5), -4.0, 4.0, (extent,), jnp.float32)
    noises = jax.random.truncated_normal(jax.random.fold_in(key, 6), -4.0, 4.0, (CHANNELS, SAMPLES), jnp.float32)
    positions = jnp.arange(SAMPLES, dtype=jnp.int32)[None, :] + delays[:, None]
    shifted = wave_trace[positions]
    return (3.0 * shared_trace[None, :] + wave_gain * shifted + gains * noises).astype(jnp.float32)


def channel_order(key):
    return jax.random.permutation(jax.random.fold_in(key, 31), CHANNELS).astype(jnp.int32)


def draw_row_channel(key, part):
    return channel_order(key)


def draw_pair_ids(key, part):
    order = channel_order(key)
    offsets = jax.random.randint(jax.random.fold_in(key, 13), (N_CHAN, 1), 0, CH_DEV)
    left_src = jax.random.randint(jax.random.fold_in(key, 11), (N_CHAN, PAIR_DEV), 0, N_CHAN)
    left_pick = jax.random.randint(jax.random.fold_in(key, 12), (N_CHAN, PAIR_DEV), 0, CAP)
    forced_src = jax.random.randint(jax.random.fold_in(key, 14), (N_CHAN, 1), 0, N_CHAN)
    slot_index = jnp.arange(PAIR_DEV, dtype=jnp.int32)[None, :]
    early = slot_index < CAP
    left_src = jnp.where(early, forced_src, left_src)
    left_pick = jnp.where(early, slot_index, left_pick)
    right_src = (left_src + jax.random.randint(jax.random.fold_in(key, 15), (N_CHAN, PAIR_DEV), 1, N_CHAN)) % N_CHAN
    right_pick = jax.random.randint(jax.random.fold_in(key, 16), (N_CHAN, PAIR_DEV), 0, CAP)
    left_rows = left_src * CH_DEV + (offsets + left_pick) % CH_DEV
    right_rows = right_src * CH_DEV + (offsets + right_pick) % CH_DEV
    left_ids = order[left_rows.reshape(-1)]
    right_ids = order[right_rows.reshape(-1)]
    return jnp.stack([left_ids, right_ids]).astype(jnp.int32)


def draw_pair_count(key, part):
    counts = jax.random.randint(jax.random.fold_in(key, 21), (N_CHAN,), 1, PAIR_DEV + 1)
    fullest = jax.random.randint(jax.random.fold_in(key, 22), (), 0, N_CHAN)
    return counts.at[fullest].set(PAIR_DEV).astype(jnp.int32)


def block_scale(key, shape, shards, least, top_value):
    loudness, own = 1.0, jax.random.fold_in(key, 6)
    for dim, shards_of in shards:
        steps = jnp.exp(jax.random.uniform(jax.random.fold_in(own, dim), (shards_of,), jnp.float32, least / len(shards), top_value / len(shards)))
        loudness = loudness * jnp.repeat(steps, shape[dim] // shards_of).reshape([-1 if axis == dim else 1 for axis in range(len(shape))])
    return loudness


def centred(stream_key, dims, spread, bound, cuts=(), held_as=jnp.bfloat16):
    factor_of = block_scale(stream_key, dims, cuts, -0.22, 0.18) if cuts else 1.0
    result = jax.random.normal(stream_key, dims, jnp.float32) * spread * factor_of
    return jnp.minimum(jnp.maximum(result, -bound), bound).astype(held_as)


def setup_inputs(seed: int = 0, part: int = 0) -> dict:
    splits = jax.random.split(jax.random.key(seed), 8)
    own_keys = jax.random.split(jax.random.fold_in(splits[7], part), 8)
    return {
        "strain": draw_strain(jax.random.fold_in(jax.random.fold_in(splits[7], part), 71), part),
        "window": centred(splits[1], (TAPS, FFT_LEN), (TAPS * FFT_LEN) ** -0.5, 0.0625, (), jnp.float32),
        "row_channel": draw_row_channel(jax.random.fold_in(jax.random.fold_in(splits[7], part), 71), part),
        "pair_ids": draw_pair_ids(jax.random.fold_in(jax.random.fold_in(splits[7], part), 71), part),
        "pair_count": draw_pair_count(jax.random.fold_in(jax.random.fold_in(splits[7], part), 71), part),
        "auto_prev": jnp.clip(jnp.exp(math.log(4.0) - 2.0794415 * jax.random.uniform(own_keys[5], (BINS, CHANNELS), jnp.float32) ** block_scale(own_keys[5], (BINS, CHANNELS), ((0, 16),), -0.2, 0.2)), 0.5, 4.0),
        "cross_prev": centred(own_keys[6], (2, BINS, PAIR_DEV), 0.5, 4.0, ((1, 16),), jnp.float32),
    }


forget_rate = 0.75


def welch(spectra, left_ids, right_ids, count, autos, previous):
    left_spec = jnp.take(spectra, left_ids, axis=2)
    right_spec = jnp.take(spectra, right_ids, axis=2)
    cross_real = jnp.mean(left_spec[0] * right_spec[0] + left_spec[1] * right_spec[1], axis=-1)
    cross_imag = jnp.mean(left_spec[1] * right_spec[0] - left_spec[0] * right_spec[1], axis=-1)
    live_slots = jnp.arange(previous.shape[-1], dtype=jnp.int32) < count
    updated = forget_rate * previous + jnp.stack([cross_real, cross_imag])
    cross_new = jnp.where(live_slots, updated, previous)
    denominator = jnp.take(autos, right_ids, axis=1)
    transfer = jnp.where(live_slots, cross_new / denominator, jnp.zeros_like(cross_new))
    return cross_new, transfer


def reference(strain, window, row_channel, pair_ids, pair_count, auto_prev, cross_prev):
    centered = strain - jnp.sum(strain, axis=0) / CHANNELS
    blocks = centered.reshape(CHANNELS, FRAMES + TAPS - 1, FFT_LEN)
    weighted = jnp.zeros((CHANNELS, FRAMES, FFT_LEN), jnp.float32)
    for tap in range(TAPS):
        weighted = weighted + window[tap] * blocks[:, tap:tap + FRAMES, :]
    transform = jnp.fft.rfft(weighted, axis=-1)[..., :BINS]
    stacked = jnp.stack([jnp.real(transform), jnp.imag(transform)]).astype(jnp.float32)
    stacked = jnp.transpose(stacked, (0, 3, 1, 2))
    inverse = jnp.zeros((CHANNELS,), jnp.int32).at[row_channel].set(jnp.arange(CHANNELS, dtype=jnp.int32))
    by_channel = jnp.take(stacked, inverse, axis=2)
    powers = jnp.mean(by_channel[0] * by_channel[0] + by_channel[1] * by_channel[1], axis=-1)
    auto_new = forget_rate * auto_prev + powers
    owned = jnp.transpose(by_channel.reshape(2, N_CHAN, BIN_DEV, CHANNELS, FRAMES), (1, 0, 2, 3, 4))
    owner_ids = jnp.transpose(pair_ids.reshape(2, N_CHAN, PAIR_DEV), (1, 0, 2))
    owner_auto = auto_new.reshape(N_CHAN, BIN_DEV, CHANNELS)
    owner_prev = jnp.transpose(cross_prev.reshape(2, N_CHAN, BIN_DEV, PAIR_DEV), (1, 0, 2, 3))

    def per_owner(items):
        spectra, ids_here, count, autos, previous = items
        return welch(spectra, ids_here[0], ids_here[1], count, autos, previous)

    cross_all, transfer_all = lax.map(per_owner, (owned, owner_ids, pair_count, owner_auto, owner_prev))
    cross_new = jnp.transpose(cross_all, (1, 0, 2, 3)).reshape(2, BINS, PAIR_DEV)
    transfer = jnp.transpose(transfer_all, (1, 0, 2, 3)).reshape(2, BINS, PAIR_DEV)
    return transfer, cross_new, auto_new
```

```python
import functools
import math

import jax
import jax.numpy as jnp
import numpy as np
from jax import lax
from jax.experimental import pallas as pl
from jax.experimental.pallas import tpu as pltpu
from jax.sharding import PartitionSpec as P

forget_rate = 0.75
LANES = 128
ROWS = 8


def make_basis(length):
    bins = length // 2
    turns = np.outer(np.arange(length), np.arange(bins)) % length
    phases = turns * (2.0 * math.pi / length)
    chunks = bins // LANES
    both = np.stack([np.cos(phases), -np.sin(phases)])
    both = both.reshape(2, length, chunks, LANES).transpose(2, 1, 0, 3).reshape(chunks, length, 2 * LANES)
    high = both.astype(jnp.bfloat16)
    low = (both - high.astype(np.float64)).astype(jnp.bfloat16)
    return high, low


def split(x):
    high = x.astype(jnp.bfloat16)
    return high, (x - high.astype(jnp.float32)).astype(jnp.bfloat16)


def spread_kernel(n, frames, taps, length, strain, window, b_high, b_low, recv, w_high, w_low, spectra, send,
                  send_sem, recv_sem, own_sem):
    me = lax.axis_index("chan")
    chunks = length // 2 // LANES
    owners = n // chunks
    width = LANES // owners
    part = frames // owners * ROWS

    barrier = pltpu.get_barrier_semaphore()

    def greet(i, carry):
        pl.semaphore_signal(barrier, inc=1, device_id={"chan": lax.rem(me + i, n)}, device_id_type=pl.DeviceIdType.MESH)
        return carry

    lax.fori_loop(1, n, greet, 0)

    step = 8
    for lane in range(0, length, LANES):
        weights = [jnp.broadcast_to(window[t : t + 1, lane : lane + LANES], (ROWS, LANES)) for t in range(taps)]

        def fir(i, carry, lane=lane, weights=weights):
            x = [
                strain[:, pl.ds(pl.multiple_of((i * step + t) * length + lane, LANES), LANES)]
                for t in range(step + taps - 1)
            ]
            rows = []
            for k in range(step):
                total = weights[0] * x[k]
                for t in range(1, taps):
                    total = total + weights[t] * x[k + t]
                rows.append(total)
            high, low = split(jnp.concatenate(rows, axis=0))
            at = pl.ds(pl.multiple_of(i * step * ROWS, step * ROWS), step * ROWS)
            w_high[at, lane : lane + LANES] = high
            w_low[at, lane : lane + LANES] = low
            return carry

        lax.fori_loop(0, frames // step, fir, 0)

    pl.semaphore_wait(barrier, n - 1)

    def remote(to):
        return pltpu.make_async_remote_copy(
            src_ref=send.at[to],
            dst_ref=recv.at[me],
            send_sem=send_sem.at[to],
            recv_sem=recv_sem.at[me],
            device_id={"chan": to},
            device_id_type=pl.DeviceIdType.MESH,
        )

    def own():
        return pltpu.make_async_copy(send.at[me], recv.at[me], own_sem)

    def chunk(j, carry):
        z = lax.rem(me // owners + chunks // 2 + j, chunks)
        high, low = b_high[z], b_low[z]
        dot = functools.partial(jnp.dot, preferred_element_type=jnp.float32)
        spectra[...] = dot(w_high[...], high) + (dot(w_high[...], low) + dot(w_low[...], high))
        group = lax.broadcasted_iota(jnp.int32, (part, LANES), 1) // width
        for ri in range(2):
            a = [spectra[q * part : (q + 1) * part, ri * LANES : (ri + 1) * LANES] for q in range(owners)]
            s = 1
            while s < owners:
                first = (group // s) % 2 == 0
                b = list(a)
                for q in range(owners):
                    if not q & s:
                        b[q] = jnp.where(first, a[q], pltpu.roll(a[q + s], s * width, 1))
                        b[q + s] = jnp.where(first, pltpu.roll(a[q], LANES - s * width, 1), a[q + s])
                a = b
                s *= 2
            for o in range(owners):
                send[z * owners + o, ri] = a[o]

        def go(o, carry):
            to = z * owners + o

            @pl.when(to != me)
            def _():
                remote(to).start()

            @pl.when(to == me)
            def _():
                own().start()

            return carry

        lax.fori_loop(0, owners, go, 0)
        return carry

    lax.fori_loop(0, chunks, chunk, 0)

    def finish(i, carry):
        other = lax.rem(me + i, n)
        pltpu.make_async_remote_copy(
            src_ref=send.at[other],
            dst_ref=recv.at[other],
            send_sem=send_sem.at[other],
            recv_sem=recv_sem.at[other],
            device_id={"chan": other},
            device_id_type=pl.DeviceIdType.MESH,
        ).wait()
        return carry

    own().wait()
    lax.fori_loop(1, n, finish, 0)


def pairs_kernel(n, frames, owners, recv, row_s, row_v, ids_s, ids_v, count, auto_prev, cross_prev,
                 transfer, cross_new, auto_new, centred, power, cross, inverse):
    channels = n * ROWS
    slots = cross_prev.shape[-1]
    width = LANES // owners
    parts = frames // owners
    part = parts * ROWS
    exact = functools.partial(
        lax.dot_general, precision=lax.Precision.HIGHEST, preferred_element_type=jnp.float32
    )

    def place(r, carry):
        inverse[row_s[r]] = r
        return carry

    lax.fori_loop(0, channels, place, 0)

    def total(s, carry):
        return carry[0] + recv[s, 0], carry[1] + recv[s, 1]

    zero = jnp.zeros((part, LANES), jnp.float32)
    sums = lax.fori_loop(0, n, total, (zero, zero))

    def mean_of(x):
        x = jnp.sum(x.reshape(parts, ROWS, LANES), axis=1, keepdims=True) * (1.0 / channels)
        return jnp.broadcast_to(x, (parts, ROWS, LANES)).reshape(part, LANES)

    means = [mean_of(x) for x in sums]

    def centre(s, carry):
        squares = jnp.zeros((ROWS, LANES), jnp.float32)
        for ri in range(2):
            x = recv[s, ri] - means[ri]
            centred[pl.ds(pl.multiple_of((s * 2 + ri) * part, part), part), :] = x
            squares = squares + jnp.sum((x * x).reshape(parts, ROWS, LANES), axis=0)
        power[pl.ds(pl.multiple_of(s * ROWS, ROWS), ROWS), :] = squares
        return carry

    lax.fori_loop(0, n, centre, 0)

    def spectrum(channel):
        row = inverse[channel]
        base = (row // ROWS) * (2 * part) + row % ROWS
        return [centred[pl.ds(base + ri * part, parts, stride=ROWS), :] for ri in range(2)]

    def pair(p, carry):
        xr, xi = spectrum(ids_s[0, p])
        yr, yi = spectrum(ids_s[1, p])
        cross[0, pl.ds(p, 1), :] = jnp.sum(xr * yr + xi * yi, axis=0, keepdims=True)
        cross[1, pl.ds(p, 1), :] = jnp.sum(xi * yr - xr * yi, axis=0, keepdims=True)
        return carry

    lax.fori_loop(0, slots, pair, 0, unroll=4)

    bin_of = lax.broadcasted_iota(jnp.int32, (width, LANES), 1) % width
    fold = jnp.where(bin_of == lax.broadcasted_iota(jnp.int32, (width, LANES), 0), 1.0 / frames, 0.0)
    by_row = exact(fold, power[...], (((1,), (1,)), ((), ())))
    names = lax.broadcasted_iota(jnp.int32, (channels, channels), 1)
    to_channel = jnp.where(names == row_v[...], 1.0, 0.0)
    autos = forget_rate * auto_prev[...] + exact(by_row, to_channel, (((1,), (0,)), ((), ())))
    auto_new[...] = autos
    right = jnp.where(lax.broadcasted_iota(jnp.int32, (channels, slots), 0) == ids_v[1:2, :], 1.0, 0.0)
    below = exact(autos, right, (((1,), (0,)), ((), ())))
    live = lax.broadcasted_iota(jnp.int32, (width, slots), 1) < count[0]
    for ri in range(2):
        term = exact(fold, cross[ri], (((1,), (1,)), ((), ())))
        previous = cross_prev[ri]
        updated = jnp.where(live, forget_rate * previous + term, previous)
        cross_new[ri] = updated
        transfer[ri] = jnp.where(live, updated / below, 0.0)


def body(strain, window, row_channel, pair_ids, pair_count, auto_prev, cross_prev):
    n = lax.axis_size("chan")
    rows, samples = strain.shape
    taps, length = window.shape
    frames = samples // length - taps + 1
    chunks = length // 2 // LANES
    owners = n // chunks
    part = frames // owners * ROWS
    channels = n * rows
    slots = pair_ids.shape[1]
    high, low = make_basis(length)
    vmem = pl.BlockSpec(memory_space=pltpu.VMEM)
    smem = pl.BlockSpec(memory_space=pltpu.SMEM)
    recv = pl.pallas_call(
        functools.partial(spread_kernel, n, frames, taps, length),
        out_shape=jax.ShapeDtypeStruct((n, 2, part, LANES), jnp.float32),
        in_specs=[vmem] * 4,
        out_specs=pl.BlockSpec(memory_space=pl.ANY),
        scratch_shapes=[
            pltpu.VMEM((frames * ROWS, length), jnp.bfloat16),
            pltpu.VMEM((frames * ROWS, length), jnp.bfloat16),
            pltpu.VMEM((frames * ROWS, 2 * LANES), jnp.float32),
            pltpu.VMEM((n, 2, part, LANES), jnp.float32),
            pltpu.SemaphoreType.DMA((n,)),
            pltpu.SemaphoreType.DMA((n,)),
            pltpu.SemaphoreType.DMA,
        ],
        compiler_params=pltpu.CompilerParams(
            collective_id=0, has_side_effects=True, vmem_limit_bytes=48 * 2**20
        ),
        name="spread",
    )(strain, window, jnp.asarray(high), jnp.asarray(low))
    return tuple(
        pl.pallas_call(
            functools.partial(pairs_kernel, n, frames, owners),
            out_shape=[
                jax.ShapeDtypeStruct(cross_prev.shape, jnp.float32),
                jax.ShapeDtypeStruct(cross_prev.shape, jnp.float32),
                jax.ShapeDtypeStruct(auto_prev.shape, jnp.float32),
            ],
            in_specs=[vmem, smem, vmem, smem, vmem, smem, vmem, vmem],
            out_specs=[vmem] * 3,
            scratch_shapes=[
                pltpu.VMEM((n * 2 * part, LANES), jnp.float32),
                pltpu.VMEM((channels, LANES), jnp.float32),
                pltpu.VMEM((2, slots, LANES), jnp.float32),
                pltpu.SMEM((channels,), jnp.int32),
            ],
            compiler_params=pltpu.CompilerParams(vmem_limit_bytes=48 * 2**20),
            name="pairs",
        )(
            recv, row_channel, row_channel.reshape(channels, 1), pair_ids, pair_ids, pair_count, auto_prev, cross_prev
        )
    )


def solution(mesh):
    in_specs = (
        P(("groups", "chan"), None),
        P(),
        P("groups"),
        P(None, ("groups", "chan")),
        P(("groups", "chan")),
        P(("groups", "chan"), None),
        P(None, ("groups", "chan"), None),
    )
    out_specs = (
        P(None, ("groups", "chan"), None),
        P(None, ("groups", "chan"), None),
        P(("groups", "chan"), None),
    )
    return jax.shard_map(body, mesh=mesh, in_specs=in_specs, out_specs=out_specs, check_vma=False)
```

```python
import functools
import math

import jax
import jax.numpy as jnp
import numpy as np
from jax import lax
from jax.experimental import pallas as pl
from jax.experimental.pallas import tpu as pltpu
from jax.sharding import PartitionSpec as P

forget_rate = 0.75
LANES = 128
ROWS = 8
CAP = 4
PLANE = 4


def make_basis(length):
    bins = length // 2
    turns = np.outer(np.arange(length), np.arange(bins)) % length
    phases = turns * (2.0 * math.pi / length)
    chunks = bins // LANES
    both = np.stack([np.cos(phases), -np.sin(phases)])
    both = both.reshape(2, length, chunks, LANES).transpose(2, 1, 0, 3).reshape(chunks, length, 2 * LANES)
    high = both.astype(jnp.bfloat16)
    low = (both - high.astype(np.float64)).astype(jnp.bfloat16)
    return high, low


def split(x):
    high = x.astype(jnp.bfloat16)
    return high, (x - high.astype(jnp.float32)).astype(jnp.bfloat16)


def spread_kernel(n, frames, taps, length, slots, strain, window, b_high, b_low, rows, ids,
                  recv, powers, mean_out, position,
                  w_high, w_low, spectra, send, wanted, asked, first, second, third, sums, own_power, turned, matches,
                  a_send, a_recv, z_send, z_recv, c_send, c_recv, g_send, g_recv, d_send, d_recv, p_send, p_recv, own_sem):
    me = lax.axis_index("chan")
    chunks = length // 2 // LANES
    owners = n // chunks
    width = LANES // owners
    group = frames // owners
    part = group * ROWS
    channels = n * ROWS
    far = n // PLANE
    plane, seat = me // PLANE, lax.rem(me, PLANE)
    piece = frames // PLANE
    dot = functools.partial(jnp.dot, preferred_element_type=jnp.float32)
    mesh_id = pl.DeviceIdType.MESH

    barrier = pltpu.get_barrier_semaphore()

    def greet(i, carry):
        pl.semaphore_signal(barrier, inc=1, device_id={"chan": lax.rem(me + i, n)}, device_id_type=mesh_id)
        return carry

    lax.fori_loop(1, n, greet, 0)

    row_name = rows[...]
    for kind in range(2):

        def match(p, carry, kind=kind):
            matches[pl.ds(kind * slots + p, 1), :] = jnp.where(row_name == ids[kind, p], 1.0, 0.0)
            return carry

        lax.fori_loop(0, slots, match, 0, unroll=8)
    named = jnp.broadcast_to(jnp.max(matches[...], axis=0, keepdims=True), (ROWS, channels))
    row_index = lax.broadcasted_iota(jnp.int32, (ROWS, channels), 1)
    within = row_index % ROWS
    rank = jnp.zeros((ROWS, channels), jnp.float32)
    for j in range(1, ROWS):
        rank = rank + jnp.where(within >= j, pltpu.roll(named, j, 1), 0.0)
    source = (row_index // ROWS).astype(jnp.float32)
    both = jnp.where(lax.broadcasted_iota(jnp.int32, (ROWS, channels), 0) == 0, source, rank)
    where = lax.dot_general(
        both.astype(jnp.bfloat16), matches[...].astype(jnp.bfloat16), (((1,), (1,)), ((), ())),
        preferred_element_type=jnp.float32,
    )
    place = where[0:1] * CAP + where[1:2]
    position[...] = jnp.broadcast_to(place, (ROWS, 2 * slots)).astype(jnp.int32)
    code = jnp.broadcast_to((named * (rank + 1.0))[0:1], (n, channels))
    mine = lax.broadcasted_iota(jnp.int32, (n, channels), 1) // ROWS == lax.broadcasted_iota(jnp.int32, (n, channels), 0)
    repeat = (
        lax.broadcasted_iota(jnp.int32, (channels, LANES), 0) % ROWS
        == lax.broadcasted_iota(jnp.int32, (channels, LANES), 1) % ROWS
    )
    codes = dot(jnp.where(mine, code, 0.0).astype(jnp.bfloat16), jnp.where(repeat, 1.0, 0.0).astype(jnp.bfloat16))
    for s in range(n):
        wanted[s] = jnp.broadcast_to(codes[s : s + 1], (ROWS, LANES))
    asked[me] = wanted[me]

    pl.semaphore_wait(barrier, n - 1)

    def copy(src, dst, out_sem, in_sem, to):
        return pltpu.make_async_remote_copy(
            src_ref=src, dst_ref=dst, send_sem=out_sem, recv_sem=in_sem, device_id={"chan": to}, device_id_type=mesh_id
        )

    def ask(i, carry):
        to = lax.rem(me + i, n)
        copy(wanted.at[to], asked.at[me], g_send.at[to], g_recv.at[me], to).start()
        return carry

    lax.fori_loop(1, n, ask, 0)

    step = 8
    for lane in range(0, length, LANES):
        weights = [jnp.broadcast_to(window[t : t + 1, lane : lane + LANES], (ROWS, LANES)) for t in range(taps)]

        def fir(i, carry, lane=lane, weights=weights):
            x = [
                strain[:, pl.ds(pl.multiple_of((i * step + t) * length + lane, LANES), LANES)]
                for t in range(step + taps - 1)
            ]
            made = []
            for k in range(step):
                total = weights[0] * x[k]
                for t in range(1, taps):
                    total = total + weights[t] * x[k + t]
                made.append(total)
            high, low = split(jnp.concatenate(made, axis=0))
            at = pl.ds(pl.multiple_of(i * step * ROWS, step * ROWS), step * ROWS)
            w_high[at, lane : lane + LANES] = high
            w_low[at, lane : lane + LANES] = low
            return carry

        lax.fori_loop(0, frames // step, fir, 0)

    adder = jnp.where(
        lax.broadcasted_iota(jnp.int32, (frames, frames * ROWS), 1) // ROWS
        == lax.broadcasted_iota(jnp.int32, (frames, frames * ROWS), 0), 1.0, 0.0
    ).astype(jnp.bfloat16)
    local = dot(adder, w_high[...]) + dot(adder, w_low[...])
    for q in range(PLANE):
        sums[q] = local[q * piece : (q + 1) * piece]
    first[seat] = sums[seat]

    def a_copy(i):
        to = lax.rem(seat + i, PLANE)
        return copy(sums.at[to], first.at[seat], a_send.at[to], a_recv.at[seat], plane * PLANE + to)

    def z_copy(i):
        to = lax.rem(plane + i, far)
        return copy(second.at[plane], second.at[plane], z_send.at[to], z_recv.at[plane], to * PLANE + seat)

    def c_copy(i):
        to = lax.rem(seat + i, PLANE)
        return copy(third.at[seat], third.at[seat], c_send.at[to], c_recv.at[seat], plane * PLANE + to)

    def arrived(buffer, out_sem, in_sem, at, to):
        copy(buffer.at[at], buffer.at[at], out_sem.at[at], in_sem.at[at], to).wait_recv()

    def start(make, count):
        def go(i, carry):
            make(i).start()
            return carry

        lax.fori_loop(1, count, go, 0)

    def spread_out(make, count):
        def go(i, carry):
            make(i).wait_send()
            return carry

        lax.fori_loop(1, count, go, 0)

    def chunk_of(j):
        return lax.rem(me // owners + chunks // 2 + j, chunks)

    def transform(j):
        z = chunk_of(j)
        high, low = b_high[z], b_low[z]
        spectra[j] = dot(w_high[...], high) + (dot(w_high[...], low) + dot(w_low[...], high))

    def turn(a, rows_of):
        lane_group = lax.broadcasted_iota(jnp.int32, (rows_of, LANES), 1) // width
        s = 1
        while s < owners:
            keep = (lane_group // s) % 2 == 0
            b = list(a)
            for q in range(owners):
                if not q & s:
                    b[q] = jnp.where(keep, a[q], pltpu.roll(a[q + s], s * width, 1))
                    b[q + s] = jnp.where(keep, pltpu.roll(a[q], LANES - s * width, 1), a[q + s])
            a = b
            s *= 2
        return a

    def d_copy(to):
        return copy(send.at[to], recv.at[me], d_send.at[to], d_recv.at[me], to)

    def own_copy():
        return pltpu.make_async_copy(send.at[me], recv.at[me], own_sem.at[0])

    def share(j):
        z = chunk_of(j)
        a = []
        for ri in range(2):
            a.append(turn([spectra[j, q * part : (q + 1) * part, ri * LANES : (ri + 1) * LANES] for q in range(owners)], part))
        same = lax.broadcasted_iota(jnp.int32, (group, part), 1) // ROWS == lax.broadcasted_iota(jnp.int32, (group, part), 0)
        for o in range(owners):
            choice = asked[z * owners + o][0:1, :part]
            pick = jnp.concatenate([jnp.where(same & (choice == q + 1.0), 1.0, 0.0) for q in range(CAP)], axis=0)
            pick = pick.astype(jnp.bfloat16)
            high, low = split(jnp.concatenate([a[0][o], a[1][o]], axis=1))
            picked = dot(pick, high) + dot(pick, low)
            send[z * owners + o, 0] = picked[:, :LANES]
            send[z * owners + o, 1] = picked[:, LANES:]

        def go(o, carry):
            to = z * owners + o

            @pl.when(to != me)
            def _():
                d_copy(to).start()

            @pl.when(to == me)
            def _():
                own_copy().start()

            return carry

        lax.fori_loop(0, owners, go, 0)

    start(a_copy, PLANE)
    transform(0)
    for i in range(1, PLANE):
        at = lax.rem(seat + i, PLANE)
        arrived(first, a_send, a_recv, at, plane * PLANE + at)
    second[plane] = functools.reduce(jnp.add, [first[q] for q in range(PLANE)])
    start(z_copy, far)

    def hear(i, carry):
        at = lax.rem(me + i, n)
        copy(wanted.at[at], asked.at[at], g_send.at[at], g_recv.at[at], at).wait()
        return carry

    lax.fori_loop(1, n, hear, 0)
    share(0)
    transform(1)
    share(1)
    transform(2)

    def z_wait(i, carry):
        at = lax.rem(plane + i, far)
        arrived(second, z_send, z_recv, at, at * PLANE + seat)
        return carry

    lax.fori_loop(1, far, z_wait, 0)
    total = second[0]
    for q in range(1, far):
        total = total + second[q]
    third[seat] = total * (1.0 / channels)
    start(c_copy, PLANE)
    share(2)
    transform(3)
    share(3)
    for i in range(1, PLANE):
        at = lax.rem(seat + i, PLANE)
        arrived(third, c_send, c_recv, at, plane * PLANE + at)
    mean_high, mean_low = split(jnp.concatenate([third[q] for q in range(PLANE)], axis=0))

    def p_copy(j, to):
        return copy(own_power.at[j], powers.at[me], p_send.at[to], p_recv.at[me], to)

    def own_power_copy(j):
        return pltpu.make_async_copy(own_power.at[j], powers.at[me], own_sem.at[1])

    own_chunk = chunks - chunks // 2
    for j in range(chunks):
        z = chunk_of(j)
        high, low = b_high[z], b_low[z]
        mean = dot(mean_high, high) + (dot(mean_high, low) + dot(mean_low, high))
        if j == own_chunk:
            for ri in range(2):
                a = turn([mean[q * group : (q + 1) * group, ri * LANES : (ri + 1) * LANES] for q in range(owners)], group)
                for o in range(owners):
                    turned[o, ri] = a[o]
            mean_out[...] = turned[lax.rem(me, owners)]
        squares = jnp.zeros((ROWS, 2 * LANES), jnp.float32)
        for k in range(frames):
            x = spectra[j, k * ROWS : (k + 1) * ROWS, :] - mean[k : k + 1, :]
            squares = squares + x * x
        own_power[j] = squares[:, :LANES] + squares[:, LANES:]

        def go(o, carry, j=j, z=z):
            to = z * owners + o

            @pl.when(to != me)
            def _():
                p_copy(j, to).start()

            @pl.when(to == me)
            def _():
                own_power_copy(j).start()

            return carry

        lax.fori_loop(0, owners, go, 0)

    spread_out(a_copy, PLANE)
    spread_out(z_copy, far)
    spread_out(c_copy, PLANE)

    def finish(i, carry):
        at = lax.rem(me + i, n)
        copy(send.at[at], recv.at[at], d_send.at[at], d_recv.at[at], at).wait()
        copy(own_power.at[0], powers.at[at], p_send.at[at], p_recv.at[at], at).wait()
        return carry

    own_copy().wait()
    own_power_copy(own_chunk).wait()
    lax.fori_loop(1, n, finish, 0)


def pairs_kernel(n, frames, owners, recv, powers, mean, position, rows, ids, count, auto_prev, cross_prev,
                 transfer, cross_new, auto_new, cross):
    channels = n * ROWS
    slots = cross_prev.shape[-1]
    width = LANES // owners
    group = frames // owners
    exact = functools.partial(
        lax.dot_general, precision=lax.Precision.HIGHEST, preferred_element_type=jnp.float32
    )
    means = [mean[0], mean[1]]

    def spectrum(place):
        s, q = place // CAP, place % CAP
        return [recv[s, ri, pl.ds(q * group, group), :] - means[ri] for ri in range(2)]

    def pair(p, carry):
        xr, xi = spectrum(position[0, p])
        yr, yi = spectrum(position[0, slots + p])
        cross[0, pl.ds(p, 1), :] = jnp.sum(xr * yr + xi * yi, axis=0, keepdims=True)
        cross[1, pl.ds(p, 1), :] = jnp.sum(xi * yr - xr * yi, axis=0, keepdims=True)
        return carry

    lax.fori_loop(0, slots, pair, 0, unroll=8)

    lane = lax.broadcasted_iota(jnp.int32, (width, LANES), 1)
    bin_of = lax.broadcasted_iota(jnp.int32, (width, LANES), 0)
    fold = jnp.where(lane % width == bin_of, 1.0 / frames, 0.0)
    offset = lax.rem(lax.axis_index("chan"), owners) * width
    mine = jnp.where(lane == bin_of + offset, 1.0 / frames, 0.0)
    last = (((1,), (1,)), ((), ()))
    by_row = exact(mine, powers[...].reshape(channels, LANES), last)
    to_channel = jnp.where(lax.broadcasted_iota(jnp.int32, (channels, channels), 0) == rows[...], 1.0, 0.0)
    autos = forget_rate * auto_prev[...] + exact(by_row, to_channel, last)
    auto_new[...] = autos
    right = jnp.where(lax.broadcasted_iota(jnp.int32, (channels, slots), 0) == ids[1:2, :], 1.0, 0.0)
    below = exact(autos, right, (((1,), (0,)), ((), ())))
    live = lax.broadcasted_iota(jnp.int32, (width, slots), 1) < count[0]
    for ri in range(2):
        term = exact(fold, cross[ri], last)
        previous = cross_prev[ri]
        updated = jnp.where(live, forget_rate * previous + term, previous)
        cross_new[ri] = updated
        transfer[ri] = jnp.where(live, updated / below, 0.0)


def body(strain, window, row_channel, pair_ids, pair_count, auto_prev, cross_prev):
    n = lax.axis_size("chan")
    rows, samples = strain.shape
    taps, length = window.shape
    frames = samples // length - taps + 1
    chunks = length // 2 // LANES
    owners = n // chunks
    group = frames // owners
    channels = n * rows
    slots = pair_ids.shape[1]
    high, low = make_basis(length)
    vmem = pl.BlockSpec(memory_space=pltpu.VMEM)
    smem = pl.BlockSpec(memory_space=pltpu.SMEM)
    anywhere = pl.BlockSpec(memory_space=pl.ANY)
    names = row_channel.reshape(1, channels)
    piece = (frames // PLANE, length)
    dma = pltpu.SemaphoreType.DMA
    f32 = jnp.float32
    recv, powers, mean, position = pl.pallas_call(
        functools.partial(spread_kernel, n, frames, taps, length, slots),
        out_shape=[
            jax.ShapeDtypeStruct((n, 2, CAP * group, LANES), f32),
            jax.ShapeDtypeStruct((n, ROWS, LANES), f32),
            jax.ShapeDtypeStruct((2, group, LANES), f32),
            jax.ShapeDtypeStruct((ROWS, 2 * slots), jnp.int32),
        ],
        in_specs=[vmem] * 5 + [smem],
        out_specs=[anywhere, anywhere, vmem, vmem],
        scratch_shapes=[
            pltpu.VMEM((frames * ROWS, length), jnp.bfloat16),
            pltpu.VMEM((frames * ROWS, length), jnp.bfloat16),
            pltpu.VMEM((chunks, frames * ROWS, 2 * LANES), f32),
            pltpu.VMEM((n, 2, CAP * group, LANES), f32),
            pltpu.VMEM((n, ROWS, LANES), f32),
            pltpu.VMEM((n, ROWS, LANES), f32),
            pltpu.VMEM((PLANE,) + piece, f32),
            pltpu.VMEM((n // PLANE,) + piece, f32),
            pltpu.VMEM((PLANE,) + piece, f32),
            pltpu.VMEM((PLANE,) + piece, f32),
            pltpu.VMEM((chunks, ROWS, LANES), f32),
            pltpu.VMEM((owners, 2, group, LANES), f32),
            pltpu.VMEM((2 * slots, channels), f32),
            dma((PLANE,)), dma((PLANE,)),
            dma((n // PLANE,)), dma((n // PLANE,)),
            dma((PLANE,)), dma((PLANE,)),
            dma((n,)), dma((n,)),
            dma((n,)), dma((n,)),
            dma((n,)), dma((n,)),
            dma((2,)),
        ],
        compiler_params=pltpu.CompilerParams(
            collective_id=0, has_side_effects=True, vmem_limit_bytes=48 * 2**20
        ),
        name="spread",
    )(strain, window, jnp.asarray(high), jnp.asarray(low), names, pair_ids)
    return tuple(
        pl.pallas_call(
            functools.partial(pairs_kernel, n, frames, owners),
            out_shape=[
                jax.ShapeDtypeStruct(cross_prev.shape, f32),
                jax.ShapeDtypeStruct(cross_prev.shape, f32),
                jax.ShapeDtypeStruct(auto_prev.shape, f32),
            ],
            in_specs=[vmem, vmem, vmem, smem, vmem, vmem, smem, vmem, vmem],
            out_specs=[vmem] * 3,
            scratch_shapes=[pltpu.VMEM((2, slots, LANES), f32)],
            compiler_params=pltpu.CompilerParams(vmem_limit_bytes=48 * 2**20),
            name="pairs",
        )(recv, powers, mean, position, names, pair_ids, pair_count, auto_prev, cross_prev)
    )


def solution(mesh):
    in_specs = (
        P(("groups", "chan"), None),
        P(),
        P("groups"),
        P(None, ("groups", "chan")),
        P(("groups", "chan")),
        P(("groups", "chan"), None),
        P(None, ("groups", "chan"), None),
    )
    out_specs = (
        P(None, ("groups", "chan"), None),
        P(None, ("groups", "chan"), None),
        P(("groups", "chan"), None),
    )
    return jax.shard_map(body, mesh=mesh, in_specs=in_specs, out_specs=out_specs, check_vma=False)
```

```python
import functools
import math

import jax
import jax.numpy as jnp
import numpy as np
from jax import lax
from jax.experimental import pallas as pl
from jax.experimental.pallas import tpu as pltpu
from jax.sharding import PartitionSpec as P

forget_rate = 0.75
LANES = 128
ROWS = 8
CAP = 4
PLANE = 4


def make_basis(length):
    bins = length // 2
    turns = np.outer(np.arange(length), np.arange(bins)) % length
    phases = turns * (2.0 * math.pi / length)
    chunks = bins // LANES
    both = np.stack([np.cos(phases), -np.sin(phases)])
    both = both.reshape(2, length, chunks, LANES).transpose(2, 1, 0, 3).reshape(chunks, length, 2 * LANES)
    high = both.astype(jnp.bfloat16)
    low = (both - high.astype(np.float64)).astype(jnp.bfloat16)
    return np.stack([high, low])


def split(x):
    high = x.astype(jnp.bfloat16)
    return high, (x - high.astype(jnp.float32)).astype(jnp.bfloat16)


def spread_kernel(n, frames, taps, length, slots, strain_in, window, basis_in, rows, ids,
                  recv, powers, mean_out, position,
                  strain, basis, load_sem, w_high, w_low, spectra, send, wanted, asked, first, second, third, sums, own_power, turned, matches,
                  a_send, a_recv, z_send, z_recv, c_send, c_recv, g_send, g_recv, d_send, d_recv, p_send, p_recv, own_sem):
    me = lax.axis_index("chan")
    chunks = length // 2 // LANES
    owners = n // chunks
    width = LANES // owners
    group = frames // owners
    part = group * ROWS
    channels = n * ROWS
    far = n // PLANE
    plane, seat = me // PLANE, lax.rem(me, PLANE)
    piece = frames // PLANE
    dot = functools.partial(jnp.dot, preferred_element_type=jnp.float32)
    mesh_id = pl.DeviceIdType.MESH

    loads = [
        pltpu.make_async_copy(src, dst, load_sem.at[i])
        for i, (src, dst) in enumerate([(strain_in, strain), (basis_in, basis)])
    ]
    for load in loads:
        load.start()

    barrier = pltpu.get_barrier_semaphore()

    def greet(i, carry):
        pl.semaphore_signal(barrier, inc=1, device_id={"chan": lax.rem(me + i, n)}, device_id_type=mesh_id)
        return carry

    lax.fori_loop(1, n, greet, 0)

    row_name = rows[...]
    for kind in range(2):

        def match(p, carry, kind=kind):
            matches[pl.ds(kind * slots + p, 1), :] = jnp.where(row_name == ids[kind, p], 1.0, 0.0)
            return carry

        lax.fori_loop(0, slots, match, 0, unroll=8)
    named = jnp.broadcast_to(jnp.max(matches[...], axis=0, keepdims=True), (ROWS, channels))
    row_index = lax.broadcasted_iota(jnp.int32, (ROWS, channels), 1)
    within = row_index % ROWS
    rank = jnp.zeros((ROWS, channels), jnp.float32)
    for j in range(1, ROWS):
        rank = rank + jnp.where(within >= j, pltpu.roll(named, j, 1), 0.0)
    source = (row_index // ROWS).astype(jnp.float32)
    both = jnp.where(lax.broadcasted_iota(jnp.int32, (ROWS, channels), 0) == 0, source, rank)
    where = lax.dot_general(
        both.astype(jnp.bfloat16), matches[...].astype(jnp.bfloat16), (((1,), (1,)), ((), ())),
        preferred_element_type=jnp.float32,
    )
    place = where[0:1] * CAP + where[1:2]
    position[...] = jnp.broadcast_to(place, (ROWS, 2 * slots)).astype(jnp.int32)
    code = jnp.broadcast_to((named * (rank + 1.0))[0:1], (n, channels))
    mine = lax.broadcasted_iota(jnp.int32, (n, channels), 1) // ROWS == lax.broadcasted_iota(jnp.int32, (n, channels), 0)
    repeat = (
        lax.broadcasted_iota(jnp.int32, (channels, LANES), 0) % ROWS
        == lax.broadcasted_iota(jnp.int32, (channels, LANES), 1) % ROWS
    )
    codes = dot(jnp.where(mine, code, 0.0).astype(jnp.bfloat16), jnp.where(repeat, 1.0, 0.0).astype(jnp.bfloat16))
    for s in range(n):
        wanted[s] = jnp.broadcast_to(codes[s : s + 1], (ROWS, LANES))
    asked[me] = wanted[me]

    pl.semaphore_wait(barrier, n - 1)

    def copy(src, dst, out_sem, in_sem, to):
        return pltpu.make_async_remote_copy(
            src_ref=src, dst_ref=dst, send_sem=out_sem, recv_sem=in_sem, device_id={"chan": to}, device_id_type=mesh_id
        )

    def ask(i, carry):
        to = lax.rem(me + i, n)
        copy(wanted.at[to], asked.at[me], g_send.at[to], g_recv.at[me], to).start()
        return carry

    lax.fori_loop(1, n, ask, 0)

    loads[0].wait()
    step = 8
    for lane in range(0, length, LANES):
        weights = [jnp.broadcast_to(window[t : t + 1, lane : lane + LANES], (ROWS, LANES)) for t in range(taps)]

        def fir(i, carry, lane=lane, weights=weights):
            x = [
                strain[:, pl.ds(pl.multiple_of((i * step + t) * length + lane, LANES), LANES)]
                for t in range(step + taps - 1)
            ]
            made = []
            for k in range(step):
                total = weights[0] * x[k]
                for t in range(1, taps):
                    total = total + weights[t] * x[k + t]
                made.append(total)
            high, low = split(jnp.concatenate(made, axis=0))
            at = pl.ds(pl.multiple_of(i * step * ROWS, step * ROWS), step * ROWS)
            w_high[at, lane : lane + LANES] = high
            w_low[at, lane : lane + LANES] = low
            return carry

        lax.fori_loop(0, frames // step, fir, 0)

    loads[1].wait()

    adder = jnp.where(
        lax.broadcasted_iota(jnp.int32, (frames, frames * ROWS), 1) // ROWS
        == lax.broadcasted_iota(jnp.int32, (frames, frames * ROWS), 0), 1.0, 0.0
    ).astype(jnp.bfloat16)
    local = dot(adder, w_high[...]) + dot(adder, w_low[...])
    for q in range(PLANE):
        sums[q] = local[q * piece : (q + 1) * piece]
    first[seat] = sums[seat]

    def a_copy(i):
        to = lax.rem(seat + i, PLANE)
        return copy(sums.at[to], first.at[seat], a_send.at[to], a_recv.at[seat], plane * PLANE + to)

    def z_copy(i):
        to = lax.rem(plane + i, far)
        return copy(second.at[plane], second.at[plane], z_send.at[to], z_recv.at[plane], to * PLANE + seat)

    def c_copy(i):
        to = lax.rem(seat + i, PLANE)
        return copy(third.at[seat], third.at[seat], c_send.at[to], c_recv.at[seat], plane * PLANE + to)

    def arrived(buffer, out_sem, in_sem, at, to):
        copy(buffer.at[at], buffer.at[at], out_sem.at[at], in_sem.at[at], to).wait_recv()

    def start(make, count):
        def go(i, carry):
            make(i).start()
            return carry

        lax.fori_loop(1, count, go, 0)

    def spread_out(make, count):
        def go(i, carry):
            make(i).wait_send()
            return carry

        lax.fori_loop(1, count, go, 0)

    def chunk_of(j):
        mine_z, half = me // owners, chunks // 2
        side = mine_z // half
        if j < half:
            return (1 - side) * half + lax.rem(mine_z + j, half)
        return side * half + lax.rem(mine_z + 1 + j, half)

    def transform(j):
        z = chunk_of(j)
        high, low = basis[0, z], basis[1, z]
        spectra[j] = dot(w_high[...], high) + (dot(w_high[...], low) + dot(w_low[...], high))

    def turn(a, rows_of):
        lane_group = lax.broadcasted_iota(jnp.int32, (rows_of, LANES), 1) // width
        s = 1
        while s < owners:
            keep = (lane_group // s) % 2 == 0
            b = list(a)
            for q in range(owners):
                if not q & s:
                    b[q] = jnp.where(keep, a[q], pltpu.roll(a[q + s], s * width, 1))
                    b[q + s] = jnp.where(keep, pltpu.roll(a[q], LANES - s * width, 1), a[q + s])
            a = b
            s *= 2
        return a

    def d_copy(to):
        return copy(send.at[to], recv.at[me], d_send.at[to], d_recv.at[me], to)

    def own_copy():
        return pltpu.make_async_copy(send.at[me], recv.at[me], own_sem.at[0])

    def share(j):
        z = chunk_of(j)
        a = []
        for ri in range(2):
            a.append(turn([spectra[j, q * part : (q + 1) * part, ri * LANES : (ri + 1) * LANES] for q in range(owners)], part))
        same = lax.broadcasted_iota(jnp.int32, (group, part), 1) // ROWS == lax.broadcasted_iota(jnp.int32, (group, part), 0)
        for o in range(owners):
            choice = asked[z * owners + o][0:1, :part]
            pick = jnp.concatenate([jnp.where(same & (choice == q + 1.0), 1.0, 0.0) for q in range(CAP)], axis=0)
            pick = pick.astype(jnp.bfloat16)
            high, low = split(jnp.concatenate([a[0][o], a[1][o]], axis=1))
            picked = dot(pick, high) + dot(pick, low)
            send[z * owners + o, 0] = picked[:, :LANES]
            send[z * owners + o, 1] = picked[:, LANES:]

        def go(o, carry):
            to = z * owners + o

            @pl.when(to != me)
            def _():
                d_copy(to).start()

            @pl.when(to == me)
            def _():
                own_copy().start()

            return carry

        lax.fori_loop(0, owners, go, 0)

    start(a_copy, PLANE)
    transform(0)
    for i in range(1, PLANE):
        at = lax.rem(seat + i, PLANE)
        arrived(first, a_send, a_recv, at, plane * PLANE + at)
    second[plane] = functools.reduce(jnp.add, [first[q] for q in range(PLANE)])
    start(z_copy, far)

    def hear(i, carry):
        at = lax.rem(me + i, n)
        copy(wanted.at[at], asked.at[at], g_send.at[at], g_recv.at[at], at).wait()
        return carry

    lax.fori_loop(1, n, hear, 0)
    transform(1)

    def z_wait(i, carry):
        at = lax.rem(plane + i, far)
        arrived(second, z_send, z_recv, at, at * PLANE + seat)
        return carry

    lax.fori_loop(1, far, z_wait, 0)
    total = second[0]
    for q in range(1, far):
        total = total + second[q]
    third[seat] = total * (1.0 / channels)
    start(c_copy, PLANE)
    share(0)
    share(1)
    transform(2)
    share(2)
    transform(3)
    share(3)
    for i in range(1, PLANE):
        at = lax.rem(seat + i, PLANE)
        arrived(third, c_send, c_recv, at, plane * PLANE + at)
    mean_high, mean_low = split(jnp.concatenate([third[q] for q in range(PLANE)], axis=0))

    def p_copy(j, to):
        return copy(own_power.at[j], powers.at[me], p_send.at[to], p_recv.at[me], to)

    def own_power_copy(j):
        return pltpu.make_async_copy(own_power.at[j], powers.at[me], own_sem.at[1])

    own_chunk = chunks - 1
    for j in range(chunks):
        z = chunk_of(j)
        high, low = basis[0, z], basis[1, z]
        mean = dot(mean_high, high) + (dot(mean_high, low) + dot(mean_low, high))
        if j == own_chunk:
            for ri in range(2):
                a = turn([mean[q * group : (q + 1) * group, ri * LANES : (ri + 1) * LANES] for q in range(owners)], group)
                for o in range(owners):
                    turned[o, ri] = a[o]
            mean_out[...] = turned[lax.rem(me, owners)]
        squares = jnp.zeros((ROWS, 2 * LANES), jnp.float32)
        for k in range(frames):
            x = spectra[j, k * ROWS : (k + 1) * ROWS, :] - mean[k : k + 1, :]
            squares = squares + x * x
        own_power[j] = squares[:, :LANES] + squares[:, LANES:]

        def go(o, carry, j=j, z=z):
            to = z * owners + o

            @pl.when(to != me)
            def _():
                p_copy(j, to).start()

            @pl.when(to == me)
            def _():
                own_power_copy(j).start()

            return carry

        lax.fori_loop(0, owners, go, 0)

    spread_out(a_copy, PLANE)
    spread_out(z_copy, far)
    spread_out(c_copy, PLANE)

    def finish(i, carry):
        at = lax.rem(me + i, n)
        copy(send.at[at], recv.at[at], d_send.at[at], d_recv.at[at], at).wait()
        copy(own_power.at[0], powers.at[at], p_send.at[at], p_recv.at[at], at).wait()
        return carry

    own_copy().wait()
    own_power_copy(own_chunk).wait()
    lax.fori_loop(1, n, finish, 0)


def pairs_kernel(n, frames, owners, recv, powers, mean, position, rows, ids, count, auto_prev, cross_prev,
                 transfer, cross_new, auto_new, cross):
    channels = n * ROWS
    slots = cross_prev.shape[-1]
    width = LANES // owners
    group = frames // owners
    exact = functools.partial(
        lax.dot_general, precision=lax.Precision.HIGHEST, preferred_element_type=jnp.float32
    )
    means = [mean[0], mean[1]]

    def spectrum(place):
        s, q = place // CAP, place % CAP
        return [recv[s, ri, pl.ds(q * group, group), :] - means[ri] for ri in range(2)]

    def pair(p, carry):
        xr, xi = spectrum(position[0, p])
        yr, yi = spectrum(position[0, slots + p])
        cross[0, pl.ds(p, 1), :] = jnp.sum(xr * yr + xi * yi, axis=0, keepdims=True)
        cross[1, pl.ds(p, 1), :] = jnp.sum(xi * yr - xr * yi, axis=0, keepdims=True)
        return carry

    lax.fori_loop(0, slots, pair, 0, unroll=8)

    lane = lax.broadcasted_iota(jnp.int32, (width, LANES), 1)
    bin_of = lax.broadcasted_iota(jnp.int32, (width, LANES), 0)
    fold = jnp.where(lane % width == bin_of, 1.0 / frames, 0.0)
    offset = lax.rem(lax.axis_index("chan"), owners) * width
    mine = jnp.where(lane == bin_of + offset, 1.0 / frames, 0.0)
    last = (((1,), (1,)), ((), ()))
    by_row = exact(mine, powers[...].reshape(channels, LANES), last)
    to_channel = jnp.where(lax.broadcasted_iota(jnp.int32, (channels, channels), 0) == rows[...], 1.0, 0.0)
    autos = forget_rate * auto_prev[...] + exact(by_row, to_channel, last)
    auto_new[...] = autos
    right = jnp.where(lax.broadcasted_iota(jnp.int32, (channels, slots), 0) == ids[1:2, :], 1.0, 0.0)
    below = exact(autos, right, (((1,), (0,)), ((), ())))
    live = lax.broadcasted_iota(jnp.int32, (width, slots), 1) < count[0]
    for ri in range(2):
        term = exact(fold, cross[ri], last)
        previous = cross_prev[ri]
        updated = jnp.where(live, forget_rate * previous + term, previous)
        cross_new[ri] = updated
        transfer[ri] = jnp.where(live, updated / below, 0.0)


def body(strain, window, row_channel, pair_ids, pair_count, auto_prev, cross_prev):
    n = lax.axis_size("chan")
    rows, samples = strain.shape
    taps, length = window.shape
    frames = samples // length - taps + 1
    chunks = length // 2 // LANES
    owners = n // chunks
    group = frames // owners
    channels = n * rows
    slots = pair_ids.shape[1]
    basis = make_basis(length)
    vmem = pl.BlockSpec(memory_space=pltpu.VMEM)
    smem = pl.BlockSpec(memory_space=pltpu.SMEM)
    anywhere = pl.BlockSpec(memory_space=pl.ANY)
    hbm = pl.BlockSpec(memory_space=pltpu.HBM)
    names = row_channel.reshape(1, channels)
    piece = (frames // PLANE, length)
    dma = pltpu.SemaphoreType.DMA
    f32 = jnp.float32
    recv, powers, mean, position = pl.pallas_call(
        functools.partial(spread_kernel, n, frames, taps, length, slots),
        out_shape=[
            jax.ShapeDtypeStruct((n, 2, CAP * group, LANES), f32),
            jax.ShapeDtypeStruct((n, ROWS, LANES), f32),
            jax.ShapeDtypeStruct((2, group, LANES), f32),
            jax.ShapeDtypeStruct((ROWS, 2 * slots), jnp.int32),
        ],
        in_specs=[hbm, vmem, hbm, vmem, smem],
        out_specs=[anywhere, anywhere, vmem, vmem],
        scratch_shapes=[
            pltpu.VMEM(strain.shape, f32),
            pltpu.VMEM(basis.shape, jnp.bfloat16),
            dma((2,)),
            pltpu.VMEM((frames * ROWS, length), jnp.bfloat16),
            pltpu.VMEM((frames * ROWS, length), jnp.bfloat16),
            pltpu.VMEM((chunks, frames * ROWS, 2 * LANES), f32),
            pltpu.VMEM((n, 2, CAP * group, LANES), f32),
            pltpu.VMEM((n, ROWS, LANES), f32),
            pltpu.VMEM((n, ROWS, LANES), f32),
            pltpu.VMEM((PLANE,) + piece, f32),
            pltpu.VMEM((n // PLANE,) + piece, f32),
            pltpu.VMEM((PLANE,) + piece, f32),
            pltpu.VMEM((PLANE,) + piece, f32),
            pltpu.VMEM((chunks, ROWS, LANES), f32),
            pltpu.VMEM((owners, 2, group, LANES), f32),
            pltpu.VMEM((2 * slots, channels), f32),
            dma((PLANE,)), dma((PLANE,)),
            dma((n // PLANE,)), dma((n // PLANE,)),
            dma((PLANE,)), dma((PLANE,)),
            dma((n,)), dma((n,)),
            dma((n,)), dma((n,)),
            dma((n,)), dma((n,)),
            dma((2,)),
        ],
        compiler_params=pltpu.CompilerParams(
            collective_id=0, has_side_effects=True, vmem_limit_bytes=60 * 2**20
        ),
        name="spread",
    )(strain, window, jnp.asarray(basis), names, pair_ids)
    return tuple(
        pl.pallas_call(
            functools.partial(pairs_kernel, n, frames, owners),
            out_shape=[
                jax.ShapeDtypeStruct(cross_prev.shape, f32),
                jax.ShapeDtypeStruct(cross_prev.shape, f32),
                jax.ShapeDtypeStruct(auto_prev.shape, f32),
            ],
            in_specs=[vmem, vmem, vmem, smem, vmem, vmem, smem, vmem, vmem],
            out_specs=[vmem] * 3,
            scratch_shapes=[pltpu.VMEM((2, slots, LANES), f32)],
            compiler_params=pltpu.CompilerParams(vmem_limit_bytes=48 * 2**20),
            name="pairs",
        )(recv, powers, mean, position, names, pair_ids, pair_count, auto_prev, cross_prev)
    )


def solution(mesh):
    in_specs = (
        P(("groups", "chan"), None),
        P(),
        P("groups"),
        P(None, ("groups", "chan")),
        P(("groups", "chan")),
        P(("groups", "chan"), None),
        P(None, ("groups", "chan"), None),
    )
    out_specs = (
        P(None, ("groups", "chan"), None),
        P(None, ("groups", "chan"), None),
        P(("groups", "chan"), None),
    )
    return jax.shard_map(body, mesh=mesh, in_specs=in_specs, out_specs=out_specs, check_vma=False)
```
